32 devices in a mesh: prompt: 8 (over y, x, core), ctx: 4 (over z).
Axes of the slice: x: 2, y: 2, z: 4, core: 2. Of those that a mesh axis runs over, the one named last changes fastest.
Arguments:
- prefix_qkv: bfloat16 [8, 512, 768], P('prompt', 'ctx'), may hold values from -8 to 8
- rollout: bfloat16 [8, 4, 8, 128, 768], P('prompt', 'ctx'), may hold values from -8 to 8
- arrival_order: int32 [8, 4, 1024], P('prompt', 'ctx'), may hold values from 0 to 1023, each once within a row
- resp_len: int32 [8, 8], P('prompt', 'ctx'), may hold values from 1 to 512, 2560 in all within a row
Outputs:
- prefix_out: bfloat16 [8, 512, 512], P('prompt', 'ctx')
- resp_out: bfloat16 [8, 8, 512, 512], P('prompt', 'ctx')
The draws below stay inside these ranges and needn't reach their ends.
All inputs are finite; a program needn't handle non-finite values. No bound on the sum of `resp_len` on one device may be relied on, other than what follows from the above.
Results may differ from the reference program's by a relative error of at most 0.0075.
Values may be sent and summed in bfloat16 or wider, within the bound.
No kernel may reach another device: no remote copies, remote signals or barrier semaphores. Data moves between devices by JAX's collectives and lax.ppermute only.
A program may use at most 64 MiB of HBM per device.

```python
import math
import jax
import jax.numpy as jnp
import numpy as np
from jax import lax

HEAD = 128
HEADS = 4
SLOT = 512
RESP_DEV = 2
PREFIX = 512
RESPONSES = 8
FEAT = 768
ROWS_PEER = 128
N_PROMPT = 8
N_CTX = 4


def draw_prefix_qkv(key, part):
    array_shape = (N_PROMPT, PREFIX, (HEADS + 2) * HEAD)
    return jax.random.truncated_normal(jax.random.fold_in(key, 2), -6.0, 6.0, array_shape, jnp.float32).astype(jnp.bfloat16)


def draw_rollout(key, part):
    array_shape = (N_PROMPT, N_CTX, N_PROMPT, ROWS_PEER, (HEADS + 2) * HEAD)
    return jax.random.truncated_normal(jax.random.fold_in(key, 4), -6.0, 6.0, array_shape, jnp.float32).astype(jnp.bfloat16)


def length_profile(amount, total, reach, lean):
    loads = [(1 << 20) // math.isqrt(rank ** lean) + 1 for rank in range(2, amount + 1)]
    rest, holding = total - reach - (amount - 1), [1] * (amount - 1)
    while rest > 0:
        movable = [i for i in range(amount - 1) if holding[i] < reach]
        mass, left = sum([loads[i] for i in movable]), rest
        for i in movable:
            extra = min(reach - holding[i], max(1, left * loads[i] // mass), rest)
            holding[i] = holding[i] + extra
            rest = rest - extra
    return np.array([reach] + holding)


def ragged_sizes(rng, amount, total, bound, skew):
    if amount == 2:
        one = jax.random.randint(rng, (), max(1, total - bound), min(bound, total - 1) + 1)
        return jnp.stack([one, total - one])
    sizes = jnp.asarray(length_profile(amount, total, bound, skew), jnp.int32)
    pairs = (amount - 1) // 2
    giver, sink = sizes[1:1 + 2 * pairs:2], sizes[2:2 + 2 * pairs:2]
    slack = jnp.minimum(giver - 1, bound - sink)
    shifted = jax.random.randint(jax.random.fold_in(rng, 1), (pairs,), 0, 1 << 20) % (slack + 1)
    sizes = sizes.at[1:1 + 2 * pairs:2].set(giver - shifted).at[2:2 + 2 * pairs:2].set(sink + shifted)
    return sizes[jax.random.permutation(jax.random.fold_in(rng, 2), amount)]


def setup_inputs(seed: int = 0) -> dict:
    arg_keys = jax.random.split(jax.random.key(seed), 5)
    return {
        "prefix_qkv": draw_prefix_qkv(jax.random.fold_in(arg_keys[4], 71), 0),
        "rollout": draw_rollout(jax.random.fold_in(arg_keys[4], 71), 0),
        "arrival_order": jax.vmap(lambda own: jax.random.permutation(own, RESP_DEV * SLOT))(jax.random.split(arg_keys[2], N_PROMPT * N_CTX)).reshape((N_PROMPT, N_CTX, RESP_DEV * SLOT)).astype(jnp.int32),
        "resp_len": jax.vmap(lambda own: ragged_sizes(own, RESPONSES, N_CTX * RESP_DEV * 5 // 8 * SLOT, SLOT, 2))(jax.random.split(arg_keys[3], N_PROMPT)).reshape((N_PROMPT, RESPONSES)).astype(jnp.int32),
    }


MASKED_SCORE = -1e30


def attend(queries, key_rows, values, allowed):
    row_count = queries.shape[0]
    head_size = key_rows.shape[1]
    head_count = queries.shape[1] // head_size
    q_heads = queries.reshape(row_count, head_count, head_size).astype(jnp.float32)
    scores = jnp.einsum("rhd,kd->hrk", q_heads, key_rows.astype(jnp.float32)) * (head_size ** -0.5)
    scores = jnp.where(allowed[None], scores, MASKED_SCORE)
    row_max = jnp.max(scores, axis=-1, keepdims=True)
    weights = jnp.exp(scores - row_max)
    row_sum = jnp.sum(weights, axis=-1)
    rounded = lax.optimization_barrier(weights.astype(jnp.bfloat16)).astype(jnp.float32)
    weighted = jnp.einsum("hrk,kd->hrd", rounded, values.astype(jnp.float32)) / row_sum[..., None]
    return jnp.transpose(weighted, (1, 0, 2)).reshape(row_count, head_count * head_size)


def reference(prefix_qkv, rollout, arrival_order, resp_len):
    query_span = HEADS * HEAD
    positions = jnp.arange(PREFIX)
    causal = positions[None, :] <= positions[:, None]
    own_pos = jnp.arange(SLOT)
    own_causal = own_pos[None, :] <= own_pos[:, None]
    full_mask = jnp.ones((SLOT, PREFIX), dtype=bool)
    response_mask = jnp.concatenate([full_mask, own_causal], axis=1)

    def one_prompt(prompt_item):
        prompt_index, prefix, row_order, lengths = prompt_item
        prefix_keys = prefix[:, query_span:query_span + HEAD]
        prefix_values = prefix[:, query_span + HEAD:]
        prefix_part = attend(prefix[:, :query_span], prefix_keys, prefix_values, causal).astype(jnp.bfloat16)
        sent_rows = jnp.take(rollout, prompt_index, axis=2)
        received = jnp.transpose(sent_rows, (1, 0, 2, 3)).reshape(N_CTX, RESP_DEV * SLOT, FEAT)
        placed = jax.vmap(lambda block_rows, block_order: jnp.take(block_rows, block_order, axis=0))(received, row_order)
        placed = placed.reshape(RESPONSES, SLOT, FEAT)

        def one_response(resp_item):
            resp_rows, resp_length = resp_item
            all_keys = jnp.concatenate([prefix_keys, resp_rows[:, query_span:query_span + HEAD]], axis=0)
            all_values = jnp.concatenate([prefix_values, resp_rows[:, query_span + HEAD:]], axis=0)
            weighted = attend(resp_rows[:, :query_span], all_keys, all_values, response_mask)
            live_rows = (own_pos < resp_length)[:, None]
            return jnp.where(live_rows, weighted, 0.0).astype(jnp.bfloat16)

        resp_part = lax.map(one_response, (placed, lengths))
        return prefix_part, resp_part

    prefix_out, resp_out = lax.map(one_prompt, (jnp.arange(N_PROMPT, dtype=jnp.int32), prefix_qkv, arrival_order, resp_len))
    return (prefix_out, resp_out)
```

```python
import functools
import math

import jax
import jax.numpy as jnp
from jax import lax
from jax.experimental import pallas as pl
from jax.experimental.pallas import tpu as pltpu
from jax.sharding import PartitionSpec as P

HEAD = 128
MASKED_SCORE = -1e30
EXP2_SCALE = HEAD ** (-0.5) * math.log2(math.e)
VMEM_LIMIT = 24 * 1024 * 1024


def mix(a, b):
    return lax.dot_general(a, b, (((1,), (0,)), ((), ())), preferred_element_type=jnp.float32)


def match(a, b):
    return lax.dot_general(a, b, (((1,), (1,)), ((), ())), preferred_element_type=jnp.float32)


def with_ones(values):
    return jnp.concatenate([values, jnp.ones_like(values)], axis=1)


def attend(scores, values):
    top = functools.reduce(jnp.maximum, [jnp.max(s, axis=1, keepdims=True) for s in scores])
    total = None
    for s, v in zip(scores, values):
        weights = jnp.exp2((s - top) * EXP2_SCALE).astype(jnp.bfloat16)
        part = mix(weights, v)
        total = part if total is None else total + part
    return total[:, :HEAD] / total[:, HEAD:]


def prefix_kernel(starts_ref, rows_ref, *refs):
    pieces, out_ref = refs[:-1], refs[-1]
    row_count = rows_ref.shape[0]
    heads = rows_ref.shape[1] // HEAD - 2
    row_pos = starts_ref[0] + lax.broadcasted_iota(jnp.int32, (row_count, 1), 0)
    kv = [rows_ref[:, heads * HEAD :]] + [p[...] for p in pieces]
    values = [with_ones(p[:, HEAD:]) for p in kv]
    seen = []
    for t, p in enumerate(kv):
        key_pos = starts_ref[t] + lax.broadcasted_iota(jnp.int32, (1, p.shape[0]), 1)
        seen.append(key_pos <= row_pos)
    for h in range(heads):
        q = rows_ref[:, h * HEAD : (h + 1) * HEAD]
        scores = [jnp.where(ok, match(q, p[:, :HEAD]), MASKED_SCORE) for ok, p in zip(seen, kv)]
        out_ref[:, h * HEAD : (h + 1) * HEAD] = attend(scores, values).astype(jnp.bfloat16)


def prefix_attention(starts, rows, pieces):
    row_count, feat = rows.shape
    return pl.pallas_call(
        prefix_kernel,
        out_shape=jax.ShapeDtypeStruct((row_count, feat - 2 * HEAD), jnp.bfloat16),
        in_specs=[pl.BlockSpec(memory_space=pltpu.SMEM)]
        + [pl.BlockSpec(memory_space=pltpu.VMEM)] * (1 + len(pieces)),
        out_specs=pl.BlockSpec(memory_space=pltpu.VMEM),
        compiler_params=pltpu.CompilerParams(vmem_limit_bytes=VMEM_LIMIT),
        name="prefix_attention",
    )(starts, rows, *pieces)


def response_kernel(block_count, piece_count, len_ref, order_ref, *refs):
    blocks = refs[:block_count]
    pieces = refs[block_count : block_count + piece_count]
    out_ref = refs[block_count + piece_count]
    arrived_ref, pk_ref, pv_ref = refs[block_count + piece_count + 1 :]
    slot = order_ref.shape[0]
    feat = arrived_ref.shape[1]
    heads = feat // HEAD - 2
    span = heads * HEAD
    r = pl.program_id(0)

    @pl.when(r == 0)
    def _():
        first = 0
        for b in blocks:
            arrived_ref[first : first + b.shape[0], :] = b[...]
            first += b.shape[0]
        first = 0
        for p in pieces:
            pk_ref[first : first + p.shape[0], :] = p[:, :HEAD]
            pv_ref[first : first + p.shape[0], :] = with_ones(p[:, HEAD:])
            first += p.shape[0]

    arrived_count = arrived_ref.shape[0]
    chosen = lax.broadcasted_iota(jnp.int32, (slot, arrived_count), 1) == order_ref[...]
    chosen = jnp.where(chosen, 1.0, 0.0).astype(jnp.bfloat16)
    placed = mix(chosen, arrived_ref[...]).astype(jnp.bfloat16)
    own_k = placed[:, span : span + HEAD]
    own_v = with_ones(placed[:, span + HEAD :])
    step = math.gcd(slot, 256)
    causal = lax.broadcasted_iota(jnp.int32, (step, step), 1) <= lax.broadcasted_iota(
        jnp.int32, (step, step), 0
    )
    length = len_ref[r]
    for c in range(slot // step):
        low, high = c * step, (c + 1) * step
        live = low + lax.broadcasted_iota(jnp.int32, (step, 1), 0) < length
        for h in range(heads):
            q = placed[low:high, h * HEAD : (h + 1) * HEAD]
            scores = [match(q, pk_ref[...])]
            values = [pv_ref[...]]
            if c:
                scores.append(match(q, own_k[:low]))
                values.append(own_v[:low])
            scores.append(jnp.where(causal, match(q, own_k[low:high]), MASKED_SCORE))
            values.append(own_v[low:high])
            result = jnp.where(live, attend(scores, values), 0.0)
            out_ref[0, low:high, h * HEAD : (h + 1) * HEAD] = result.astype(jnp.bfloat16)


def response_attention(lengths, order, blocks, pieces):
    responses = lengths.shape[0]
    slot = order.shape[0] // responses
    feat = blocks[0].shape[1]
    arrived_count = sum(b.shape[0] for b in blocks)
    prefix_count = sum(p.shape[0] for p in pieces)
    whole = pl.BlockSpec(memory_space=pltpu.VMEM)
    return pl.pallas_call(
        functools.partial(response_kernel, len(blocks), len(pieces)),
        grid=(responses,),
        out_shape=jax.ShapeDtypeStruct((responses, slot, feat - 2 * HEAD), jnp.bfloat16),
        in_specs=[
            pl.BlockSpec(memory_space=pltpu.SMEM),
            pl.BlockSpec((slot, 1), lambda r: (r, 0)),
        ]
        + [whole] * (len(blocks) + len(pieces)),
        out_specs=pl.BlockSpec((1, slot, feat - 2 * HEAD), lambda r: (r, 0, 0)),
        scratch_shapes=[
            pltpu.VMEM((arrived_count, feat), jnp.bfloat16),
            pltpu.VMEM((prefix_count, HEAD), jnp.bfloat16),
            pltpu.VMEM((prefix_count, 2 * HEAD), jnp.bfloat16),
        ],
        compiler_params=pltpu.CompilerParams(vmem_limit_bytes=VMEM_LIMIT),
        name="response_attention",
    )(lengths, order, *blocks, *pieces)


def body(prefix_qkv, rollout, arrival_order, resp_len):
    peers = lax.axis_size("prompt")
    ctx_count = lax.axis_size("ctx")
    prompt_index = lax.axis_index("prompt")
    ctx_index = lax.axis_index("ctx")
    prefix_rows = prefix_qkv[0]
    prefix_len, feat = prefix_rows.shape
    sent = rollout[0, 0]
    rows_peer = sent.shape[1]
    assert peers & (peers - 1) == 0

    blocks = [lax.dynamic_index_in_dim(sent, prompt_index, 0, keepdims=False)]
    for k in range(1, peers):
        block = lax.dynamic_index_in_dim(sent, prompt_index ^ k, 0, keepdims=False)
        blocks.append(lax.ppermute(block, "prompt", [(j, j ^ k) for j in range(peers)]))
    order = (arrival_order[0, 0] ^ (prompt_index * rows_peer)).reshape(-1, 1)

    prefix_kv = prefix_rows[:, feat - 2 * HEAD :]
    shifted = [
        lax.ppermute(prefix_kv, "ctx", [(j, (j + t) % ctx_count) for j in range(ctx_count)])
        for t in range(1, ctx_count)
    ]
    starts = (ctx_index - jnp.arange(ctx_count, dtype=jnp.int32)) % ctx_count * prefix_len
    prefix_out = prefix_attention(starts, prefix_rows, shifted)
    resp_out = response_attention(resp_len[0], order, blocks, [prefix_kv] + shifted)
    return (prefix_out[None], resp_out[None])


def solution(mesh):
    placed = (
        P("prompt", "ctx", None),
        P("prompt", "ctx", None, None, None),
        P("prompt", "ctx", None),
        P("prompt", "ctx"),
    )
    return jax.shard_map(
        body,
        mesh=mesh,
        in_specs=placed,
        out_specs=(P("prompt", "ctx", None), P("prompt", "ctx", None, None)),
        check_vma=False,
    )
```

```python
import functools
import math

import jax
import jax.numpy as jnp
from jax import lax
from jax.experimental import pallas as pl
from jax.experimental.pallas import tpu as pltpu
from jax.sharding import PartitionSpec as P

HEAD = 128
MASKED_SCORE = -1e30
EXP2_SCALE = HEAD ** (-0.5) * math.log2(math.e)
VMEM_LIMIT = 24 * 1024 * 1024


def mix(a, b):
    return lax.dot_general(a, b, (((1,), (0,)), ((), ())), preferred_element_type=jnp.float32)


def match(a, b):
    return lax.dot_general(a, b, (((1,), (1,)), ((), ())), preferred_element_type=jnp.float32)


def with_ones(values):
    return jnp.concatenate([values, jnp.ones_like(values)], axis=1)


def attend(scores, values):
    top = functools.reduce(jnp.maximum, [jnp.max(s, axis=1, keepdims=True) for s in scores])
    total = None
    for s, v in zip(scores, values):
        weights = jnp.exp2((s - top) * EXP2_SCALE).astype(jnp.bfloat16)
        part = mix(weights, v)
        total = part if total is None else total + part
    return total[:, :HEAD] / total[:, HEAD:]


def prefix_kernel(starts_ref, rows_ref, *refs):
    pieces, out_ref = refs[:-1], refs[-1]
    row_count = rows_ref.shape[0]
    heads = rows_ref.shape[1] // HEAD - 2
    row_pos = starts_ref[0] + lax.broadcasted_iota(jnp.int32, (row_count, 1), 0)
    kv = [rows_ref[:, heads * HEAD :]] + [p[...] for p in pieces]
    values = [with_ones(p[:, HEAD:]) for p in kv]
    seen = []
    for t, p in enumerate(kv):
        key_pos = starts_ref[t] + lax.broadcasted_iota(jnp.int32, (1, p.shape[0]), 1)
        seen.append(key_pos <= row_pos)
    for h in range(heads):
        q = rows_ref[:, h * HEAD : (h + 1) * HEAD]
        scores = [jnp.where(ok, match(q, p[:, :HEAD]), MASKED_SCORE) for ok, p in zip(seen, kv)]
        out_ref[:, h * HEAD : (h + 1) * HEAD] = attend(scores, values).astype(jnp.bfloat16)


def prefix_attention(starts, rows, pieces):
    row_count, feat = rows.shape
    return pl.pallas_call(
        prefix_kernel,
        out_shape=jax.ShapeDtypeStruct((row_count, feat - 2 * HEAD), jnp.bfloat16),
        in_specs=[pl.BlockSpec(memory_space=pltpu.SMEM)]
        + [pl.BlockSpec(memory_space=pltpu.VMEM)] * (1 + len(pieces)),
        out_specs=pl.BlockSpec(memory_space=pltpu.VMEM),
        compiler_params=pltpu.CompilerParams(vmem_limit_bytes=VMEM_LIMIT),
        name="prefix_attention",
    )(starts, rows, *pieces)


def response_kernel(block_count, piece_count, len_ref, order_ref, *refs):
    blocks = refs[:block_count]
    pieces = refs[block_count : block_count + piece_count]
    out_ref = refs[block_count + piece_count]
    arrived_ref, pk_ref, pv_ref = refs[block_count + piece_count + 1 :]
    slot = order_ref.shape[0]
    feat = arrived_ref.shape[1]
    heads = feat // HEAD - 2
    span = heads * HEAD
    r = pl.program_id(0)

    @pl.when(r == 0)
    def _():
        first = 0
        for b in blocks:
            arrived_ref[first : first + b.shape[0], :] = b[...]
            first += b.shape[0]
        first = 0
        for p in pieces:
            pk_ref[first : first + p.shape[0], :] = p[:, :HEAD]
            pv_ref[first : first + p.shape[0], :] = with_ones(p[:, HEAD:])
            first += p.shape[0]

    arrived_count = arrived_ref.shape[0]
    chosen = lax.broadcasted_iota(jnp.int32, (slot, arrived_count), 1) == order_ref[...]
    chosen = jnp.where(chosen, 1.0, 0.0).astype(jnp.bfloat16)
    placed = mix(chosen, arrived_ref[...]).astype(jnp.bfloat16)
    own_k = placed[:, span : span + HEAD]
    own_v = with_ones(placed[:, span + HEAD :])
    step = math.gcd(slot, 256)
    causal = lax.broadcasted_iota(jnp.int32, (step, step), 1) <= lax.broadcasted_iota(
        jnp.int32, (step, step), 0
    )
    length = len_ref[r]
    for c in range(slot // step):
        low, high = c * step, (c + 1) * step
        live = low + lax.broadcasted_iota(jnp.int32, (step, 1), 0) < length
        for h in range(heads):
            q = placed[low:high, h * HEAD : (h + 1) * HEAD]
            scores = [match(q, pk_ref[...])]
            values = [pv_ref[...]]
            if c:
                scores.append(match(q, own_k[:low]))
                values.append(own_v[:low])
            scores.append(jnp.where(causal, match(q, own_k[low:high]), MASKED_SCORE))
            values.append(own_v[low:high])
            result = jnp.where(live, attend(scores, values), 0.0)
            out_ref[0, low:high, h * HEAD : (h + 1) * HEAD] = result.astype(jnp.bfloat16)


def response_attention(lengths, order, blocks, pieces):
    responses = lengths.shape[0]
    slot = order.shape[0] // responses
    feat = blocks[0].shape[1]
    arrived_count = sum(b.shape[0] for b in blocks)
    prefix_count = sum(p.shape[0] for p in pieces)
    whole = pl.BlockSpec(memory_space=pltpu.VMEM)
    return pl.pallas_call(
        functools.partial(response_kernel, len(blocks), len(pieces)),
        grid=(responses,),
        out_shape=jax.ShapeDtypeStruct((responses, slot, feat - 2 * HEAD), jnp.bfloat16),
        in_specs=[
            pl.BlockSpec(memory_space=pltpu.SMEM),
            pl.BlockSpec((slot, 1), lambda r: (r, 0)),
        ]
        + [whole] * (len(blocks) + len(pieces)),
        out_specs=pl.BlockSpec((1, slot, feat - 2 * HEAD), lambda r: (r, 0, 0)),
        scratch_shapes=[
            pltpu.VMEM((arrived_count, feat), jnp.bfloat16),
            pltpu.VMEM((prefix_count, HEAD), jnp.bfloat16),
            pltpu.VMEM((prefix_count, 2 * HEAD), jnp.bfloat16),
        ],
        compiler_params=pltpu.CompilerParams(vmem_limit_bytes=VMEM_LIMIT),
        name="response_attention",
    )(lengths, order, *blocks, *pieces)


def body(prefix_qkv, rollout, arrival_order, resp_len):
    peers = lax.axis_size("prompt")
    ctx_count = lax.axis_size("ctx")
    prompt_index = lax.axis_index("prompt")
    ctx_index = lax.axis_index("ctx")
    prefix_rows = prefix_qkv[0]
    prefix_len, feat = prefix_rows.shape
    sent = rollout[0, 0]
    rows_peer = sent.shape[1]
    assert peers & (peers - 1) == 0

    order = (arrival_order[0, 0] ^ (prompt_index * rows_peer)).reshape(-1, 1)

    def pick(index, k):
        return lax.dynamic_index_in_dim(sent, index ^ k, 0, keepdims=False)

    def swap(block, k):
        return lax.ppermute(block, "prompt", [(j, j ^ k) for j in range(peers)])

    def after(value, *done):
        return lax.optimization_barrier((value, *done))[0]

    ranks = sorted(range(1, peers), key=lambda k: (-(k >> 1).bit_count(), k))
    lead, rest = ranks[:2], ranks[2:]
    blocks = [None] * peers
    picked = [pick(prompt_index, k) for k in lead]
    *picked, index, prefix_kv = lax.optimization_barrier(
        (*picked, prompt_index, prefix_rows[:, feat - 2 * HEAD :])
    )
    for k, block in zip(lead, picked):
        blocks[k] = swap(block, k)
    shifted = [
        lax.ppermute(prefix_kv, "ctx", [(j, (j + t) % ctx_count) for j in range(ctx_count)])
        for t in range(1, ctx_count)
    ]
    earlier = shifted + [blocks[k] for k in lead]
    for n, k in enumerate(rest):
        block = pick(index, k)
        if n < len(earlier):
            block = after(block, earlier[n])
        blocks[k] = swap(block, k)
    blocks[0] = pick(index, 0)
    starts = (ctx_index - jnp.arange(ctx_count, dtype=jnp.int32)) % ctx_count * prefix_len
    prefix_out = prefix_attention(starts, prefix_rows, shifted)
    resp_out = response_attention(resp_len[0], order, blocks, [prefix_kv] + shifted)
    return (prefix_out[None], resp_out[None])


def solution(mesh):
    placed = (
        P("prompt", "ctx", None),
        P("prompt", "ctx", None, None, None),
        P("prompt", "ctx", None),
        P("prompt", "ctx"),
    )
    return jax.shard_map(
        body,
        mesh=mesh,
        in_specs=placed,
        out_specs=(P("prompt", "ctx", None), P("prompt", "ctx", None, None)),
        check_vma=False,
    )
```

```python
import functools
import math

import jax
import jax.numpy as jnp
from jax import lax
from jax.experimental import pallas as pl
from jax.experimental.pallas import tpu as pltpu
from jax.sharding import PartitionSpec as P

HEAD = 128
MASKED_SCORE = -1e30
EXP2_SCALE = HEAD ** (-0.5) * math.log2(math.e)
VMEM_LIMIT = 24 * 1024 * 1024


def mix(a, b):
    return lax.dot_general(a, b, (((1,), (0,)), ((), ())), preferred_element_type=jnp.float32)


def match(a, b):
    return lax.dot_general(a, b, (((1,), (1,)), ((), ())), preferred_element_type=jnp.float32)


def with_ones(values):
    return jnp.concatenate([values, jnp.ones_like(values)], axis=1)


def attend(scores, values):
    top = functools.reduce(jnp.maximum, [jnp.max(s, axis=1, keepdims=True) for s in scores])
    total = None
    for s, v in zip(scores, values):
        weights = jnp.exp2((s - top) * EXP2_SCALE).astype(jnp.bfloat16)
        part = mix(weights, v)
        total = part if total is None else total + part
    return total[:, :HEAD] / total[:, HEAD:]


def prefix_part(starts_ref, rows_ref, pk_ref, pv_ref, out_ref):
    row_count = rows_ref.shape[0]
    heads = rows_ref.shape[1] // HEAD - 2
    row_pos = starts_ref[0] + lax.broadcasted_iota(jnp.int32, (row_count, 1), 0)
    seen = []
    for first in range(0, pk_ref.shape[0], row_count):
        key_pos = starts_ref[first // row_count] + lax.broadcasted_iota(jnp.int32, (1, row_count), 1)
        seen.append(key_pos <= row_pos)
    seen = jnp.concatenate(seen, axis=1)
    seen = jnp.concatenate([seen] * heads, axis=0)
    q = jnp.concatenate([rows_ref[:, h * HEAD : (h + 1) * HEAD] for h in range(heads)], axis=0)
    scores = jnp.where(seen, match(q, pk_ref[...]), MASKED_SCORE)
    result = attend([scores], [pv_ref[...]]).astype(jnp.bfloat16)
    for h in range(heads):
        out_ref[:, h * HEAD : (h + 1) * HEAD] = result[h * row_count : (h + 1) * row_count]


def place(order_ref, arrived, r, slot):
    chosen = lax.broadcasted_iota(jnp.int32, (slot, arrived.shape[0]), 1)
    chosen = chosen == order_ref[r * slot : (r + 1) * slot, :]
    chosen = jnp.where(chosen, 1.0, 0.0).astype(jnp.bfloat16)
    return mix(chosen, arrived).astype(jnp.bfloat16)


def response_part(len_ref, queries, first_head, keys, values, pk_ref, pv_ref, hold_ref, out_ref, sems):
    slot = queries[0].shape[0]
    heads = queries[0].shape[1] // HEAD
    step = math.gcd(slot, 256)
    chunks = slot // step
    causal = lax.broadcasted_iota(jnp.int32, (step, step), 1) <= lax.broadcasted_iota(
        jnp.int32, (step, step), 0
    )
    items = [(r, c, h) for r in range(len(queries)) for c in range(chunks) for h in range(heads)]

    def scored(r, c, h):
        low, high = c * step, (c + 1) * step
        q = queries[r][low:high, h * HEAD : (h + 1) * HEAD]
        scores = [match(q, pk_ref[...])]
        if c:
            scores.append(match(q, keys[r][:low]))
        scores.append(jnp.where(causal, match(q, keys[r][low:high]), MASKED_SCORE))
        return scores

    columns = pl.ds(first_head * HEAD, heads * HEAD)
    copies = []
    ahead = scored(*items[0])
    for n, (r, c, h) in enumerate(items):
        scores = ahead
        if n + 1 < len(items):
            ahead = scored(*items[n + 1])
        low, high = c * step, (c + 1) * step
        value = [pv_ref[...]] + ([values[r][:low]] if c else []) + [values[r][low:high]]
        live = low + lax.broadcasted_iota(jnp.int32, (step, 1), 0) < len_ref[r]
        result = jnp.where(live, attend(scores, value), 0.0)
        hold_ref[r, low:high, h * HEAD : (h + 1) * HEAD] = result.astype(jnp.bfloat16)
        if h == heads - 1:
            copy = pltpu.make_async_copy(
                hold_ref.at[r, pl.ds(low, step)],
                out_ref.at[r, pl.ds(low, step), columns],
                sems.at[r, c],
            )
            copy.start()
            copies.append(copy)
    for copy in copies:
        copy.wait()


def load_prefix(pieces, pk_ref, pv_ref):
    first = 0
    for p in pieces:
        pk_ref[first : first + p.shape[0], :] = p[:, :HEAD]
        pv_ref[first : first + p.shape[0], :] = with_ones(p[:, HEAD:])
        first += p.shape[0]


def prefix_kernel(starts_ref, rows_ref, kv_ref, out_ref, pk_ref, pv_ref):
    load_prefix([kv_ref], pk_ref, pv_ref)
    prefix_part(starts_ref, rows_ref, pk_ref, pv_ref, out_ref)


def prefix_call(starts, rows, kv):
    return pl.pallas_call(
        prefix_kernel,
        out_shape=jax.ShapeDtypeStruct((rows.shape[0], rows.shape[1] - 2 * HEAD), jnp.bfloat16),
        in_specs=[SCALARS, WHOLE, WHOLE],
        out_specs=WHOLE,
        scratch_shapes=prefix_scratch(kv.shape[0]),
        compiler_params=pltpu.CompilerParams(vmem_limit_bytes=VMEM_LIMIT),
        cost_estimate=pl.CostEstimate(flops=10**9, bytes_accessed=10**6, transcendentals=0),
        name="prefix_attention",
    )(starts, rows, kv)


def response_kernel(len_ref, order_ref, sent_ref, prefix_ref, *refs):
    blocks = refs[:-7]
    out_ref, arrived_ref, pk_ref, pv_ref, hold_ref, sems, own_sem = refs[-7:]
    responses, slot, span = hold_ref.shape
    index = lax.axis_index("prompt")
    rows_peer = sent_ref.shape[1]
    first = pl.multiple_of(index * rows_peer, rows_peer)
    own = pltpu.make_async_copy(
        sent_ref.at[index], arrived_ref.at[pl.ds(first, rows_peer)], own_sem
    )
    own.start()
    load_prefix([prefix_ref], pk_ref, pv_ref)
    for k, b in enumerate(blocks, 1):
        first = pl.multiple_of((index ^ k) * rows_peer, rows_peer)
        arrived_ref[pl.ds(first, rows_peer), :] = b[...]
    own.wait()
    placed = [place(order_ref, arrived_ref[...], r, slot) for r in range(responses)]
    response_part(
        len_ref,
        [p[:, :span] for p in placed],
        0,
        [p[:, span : span + HEAD] for p in placed],
        [with_ones(p[:, span + HEAD :]) for p in placed],
        pk_ref,
        pv_ref,
        hold_ref,
        out_ref,
        sems,
    )


WHOLE = pl.BlockSpec(memory_space=pltpu.VMEM)
SCALARS = pl.BlockSpec(memory_space=pltpu.SMEM)
ANYWHERE = pl.BlockSpec(memory_space=pl.ANY)
IN_HBM = pl.BlockSpec(memory_space=pltpu.HBM)


def prefix_scratch(count):
    return [pltpu.VMEM((count, HEAD), jnp.bfloat16), pltpu.VMEM((count, 2 * HEAD), jnp.bfloat16)]


def response_call(lengths, order, sent, prefix_kv, blocks):
    responses = lengths.shape[0]
    slot = order.shape[0] // responses
    feat = sent.shape[2]
    span = feat - 2 * HEAD
    return pl.pallas_call(
        response_kernel,
        out_shape=jax.ShapeDtypeStruct((responses, slot, span), jnp.bfloat16),
        in_specs=[SCALARS, WHOLE, IN_HBM, WHOLE] + [WHOLE] * len(blocks),
        out_specs=ANYWHERE,
        scratch_shapes=[pltpu.VMEM((responses * slot, feat), jnp.bfloat16)]
        + prefix_scratch(prefix_kv.shape[0])
        + [
            pltpu.VMEM((responses, slot, span), jnp.bfloat16),
            pltpu.SemaphoreType.DMA((responses, slot // math.gcd(slot, 256))),
            pltpu.SemaphoreType.DMA,
        ],
        compiler_params=pltpu.CompilerParams(vmem_limit_bytes=VMEM_LIMIT),
        cost_estimate=pl.CostEstimate(flops=5 * 10**9, bytes_accessed=4 * 10**6, transcendentals=0),
        name="response_attention",
    )(lengths, order, sent, prefix_kv, *blocks)


def body(prefix_qkv, rollout, arrival_order, resp_len):
    peers = lax.axis_size("prompt")
    ctx_count = lax.axis_size("ctx")
    ctx_index = lax.axis_index("ctx")
    prefix_rows = prefix_qkv[0]
    prefix_len, feat = prefix_rows.shape
    sent = rollout[0, 0]
    assert peers & (peers - 1) == 0

    def after(value, *done):
        return lax.optimization_barrier((value, *done))[0]

    def pick(index, k):
        return lax.dynamic_index_in_dim(sent, index ^ k, 0, keepdims=False)

    ks = sorted(range(1, peers), key=lambda k: (-(k >> 1).bit_count(), k & 1, -k))
    first = pick(lax.axis_index("prompt"), ks[0])
    index, rows, first = lax.optimization_barrier((lax.axis_index("prompt"), prefix_rows, first))
    picked = {k: pick(index, k) for k in ks[1:]}
    picked[ks[0]] = first
    prefix_kv = rows[:, feat - 2 * HEAD :]

    swaps = [("prompt", k) for k in ks]
    shifts = [("ctx", t) for t in range(1, ctx_count)]
    plan = swaps[:3] + shifts[:2] + swaps[3:5] + shifts[2:] + swaps[5:]
    freed = plan[3:5] + plan[:3] + plan[5:]
    got = {}
    for n, (axis, by) in enumerate(plan):
        if axis == "ctx":
            value, pairs = prefix_kv, [(j, (j + by) % ctx_count) for j in range(ctx_count)]
        else:
            value, pairs = picked[by], [(j, j ^ by) for j in range(peers)]
        if n >= 5:
            value = after(value, got[freed[n - 5]])
        got[axis, by] = lax.ppermute(value, axis, pairs)
    blocks = [got["prompt", k] for k in range(1, peers)]
    prefix_kv = jnp.concatenate([prefix_kv] + [got[s] for s in shifts], axis=0)

    order = arrival_order[0, 0].reshape(-1, 1)
    starts = (ctx_index - jnp.arange(ctx_count, dtype=jnp.int32)) % ctx_count * prefix_len
    prefix_out = prefix_call(starts, prefix_rows, prefix_kv)
    resp_out = response_call(
        resp_len[0], order, sent, prefix_kv, blocks
    )
    return (prefix_out[None], resp_out[None])


def solution(mesh):
    placed = (
        P("prompt", "ctx", None),
        P("prompt", "ctx", None, None, None),
        P("prompt", "ctx", None),
        P("prompt", "ctx"),
    )
    return jax.shard_map(
        body,
        mesh=mesh,
        in_specs=placed,
        out_specs=(P("prompt", "ctx", None), P("prompt", "ctx", None, None)),
        check_vma=False,
    )
```

```python
import functools
import math

import jax
import jax.numpy as jnp
from jax import lax
from jax.experimental import pallas as pl
from jax.experimental.pallas import tpu as pltpu
from jax.sharding import PartitionSpec as P

HEAD = 128
MASKED_SCORE = -1e30
EXP2_SCALE = HEAD ** (-0.5) * math.log2(math.e)
VMEM_LIMIT = 24 * 1024 * 1024


def mix(a, b):
    return lax.dot_general(a, b, (((1,), (0,)), ((), ())), preferred_element_type=jnp.float32)


def match(a, b):
    return lax.dot_general(a, b, (((1,), (1,)), ((), ())), preferred_element_type=jnp.float32)


def with_ones(values):
    return jnp.concatenate([values, jnp.ones_like(values)], axis=1)


def attend(scores, values):
    top = functools.reduce(jnp.maximum, [jnp.max(s, axis=1, keepdims=True) for s in scores])
    total = None
    for s, v in zip(scores, values):
        weights = jnp.exp2((s - top) * EXP2_SCALE).astype(jnp.bfloat16)
        part = mix(weights, v)
        total = part if total is None else total + part
    return total[:, :HEAD] / total[:, HEAD:]


def prefix_part(starts_ref, rows_ref, pk_ref, pv_ref, out_ref):
    row_count = rows_ref.shape[0]
    heads = rows_ref.shape[1] // HEAD - 2
    row_pos = starts_ref[0] + lax.broadcasted_iota(jnp.int32, (row_count, 1), 0)
    seen = []
    for first in range(0, pk_ref.shape[0], row_count):
        key_pos = starts_ref[first // row_count] + lax.broadcasted_iota(jnp.int32, (1, row_count), 1)
        seen.append(key_pos <= row_pos)
    seen = jnp.concatenate(seen, axis=1)
    seen = jnp.concatenate([seen] * heads, axis=0)
    q = jnp.concatenate([rows_ref[:, h * HEAD : (h + 1) * HEAD] for h in range(heads)], axis=0)
    scores = jnp.where(seen, match(q, pk_ref[...]), MASKED_SCORE)
    result = attend([scores], [pv_ref[...]]).astype(jnp.bfloat16)
    for h in range(heads):
        out_ref[:, h * HEAD : (h + 1) * HEAD] = result[h * row_count : (h + 1) * row_count]


def place(order_ref, arrived, r, slot):
    chosen = lax.broadcasted_iota(jnp.int32, (slot, arrived.shape[0]), 1)
    chosen = chosen == order_ref[r * slot : (r + 1) * slot, :]
    chosen = jnp.where(chosen, 1.0, 0.0).astype(jnp.bfloat16)
    return mix(chosen, arrived).astype(jnp.bfloat16)


def response_part(len_ref, queries, first_head, keys, values, pk_ref, pv_ref, hold_ref, out_ref, sems):
    slot = queries[0].shape[0]
    heads = queries[0].shape[1] // HEAD
    step = math.gcd(slot, 256)
    chunks = slot // step
    causal = lax.broadcasted_iota(jnp.int32, (step, step), 1) <= lax.broadcasted_iota(
        jnp.int32, (step, step), 0
    )
    items = [(r, c, h) for r in range(len(queries)) for c in range(chunks) for h in range(heads)]

    def scored(r, c, h):
        low, high = c * step, (c + 1) * step
        q = queries[r][low:high, h * HEAD : (h + 1) * HEAD]
        scores = [match(q, pk_ref[...])]
        if c:
            scores.append(match(q, keys[r][:low]))
        scores.append(jnp.where(causal, match(q, keys[r][low:high]), MASKED_SCORE))
        return scores

    columns = pl.ds(first_head * HEAD, heads * HEAD)
    copies = []
    ahead = scored(*items[0])
    for n, (r, c, h) in enumerate(items):
        scores = ahead
        if n + 1 < len(items):
            ahead = scored(*items[n + 1])
        low, high = c * step, (c + 1) * step
        value = [pv_ref[...]] + ([values[r][:low]] if c else []) + [values[r][low:high]]
        live = low + lax.broadcasted_iota(jnp.int32, (step, 1), 0) < len_ref[r]
        result = jnp.where(live, attend(scores, value), 0.0)
        hold_ref[r, low:high, h * HEAD : (h + 1) * HEAD] = result.astype(jnp.bfloat16)
        if h == heads - 1:
            copy = pltpu.make_async_copy(
                hold_ref.at[r, pl.ds(low, step)],
                out_ref.at[r, pl.ds(low, step), columns],
                sems.at[r, c],
            )
            copy.start()
            copies.append(copy)
    for copy in copies:
        copy.wait()


def load_prefix(pieces, pk_ref, pv_ref):
    first = 0
    for p in pieces:
        pk_ref[first : first + p.shape[0], :] = p[:, :HEAD]
        pv_ref[first : first + p.shape[0], :] = with_ones(p[:, HEAD:])
        first += p.shape[0]


def prefix_kernel(starts_ref, rows_ref, kv_ref, out_ref, pk_ref, pv_ref):
    load_prefix([kv_ref], pk_ref, pv_ref)
    prefix_part(starts_ref, rows_ref, pk_ref, pv_ref, out_ref)


def prefix_call(starts, rows, kv):
    return pl.pallas_call(
        prefix_kernel,
        out_shape=jax.ShapeDtypeStruct((rows.shape[0], rows.shape[1] - 2 * HEAD), jnp.bfloat16),
        in_specs=[SCALARS, WHOLE, WHOLE],
        out_specs=WHOLE,
        scratch_shapes=prefix_scratch(kv.shape[0]),
        compiler_params=pltpu.CompilerParams(vmem_limit_bytes=VMEM_LIMIT),
        cost_estimate=pl.CostEstimate(flops=10**9, bytes_accessed=10**6, transcendentals=0),
        name="prefix_attention",
    )(starts, rows, kv)


def response_kernel(len_ref, order_ref, sent_ref, prefix_ref, *refs):
    blocks = refs[:-7]
    out_ref, arrived_ref, pk_ref, pv_ref, hold_ref, sems, own_sem = refs[-7:]
    responses, slot, span = hold_ref.shape
    index = lax.axis_index("prompt")
    rows_peer = sent_ref.shape[1]
    first = pl.multiple_of(index * rows_peer, rows_peer)
    own = pltpu.make_async_copy(
        sent_ref.at[index], arrived_ref.at[pl.ds(first, rows_peer)], own_sem
    )
    own.start()
    load_prefix([prefix_ref], pk_ref, pv_ref)
    for k, b in enumerate(blocks, 1):
        first = pl.multiple_of((index ^ k) * rows_peer, rows_peer)
        arrived_ref[pl.ds(first, rows_peer), :] = b[...]
    own.wait()
    placed = [place(order_ref, arrived_ref[...], r, slot) for r in range(responses)]
    response_part(
        len_ref,
        [p[:, :span] for p in placed],
        0,
        [p[:, span : span + HEAD] for p in placed],
        [with_ones(p[:, span + HEAD :]) for p in placed],
        pk_ref,
        pv_ref,
        hold_ref,
        out_ref,
        sems,
    )


WHOLE = pl.BlockSpec(memory_space=pltpu.VMEM)
SCALARS = pl.BlockSpec(memory_space=pltpu.SMEM)
ANYWHERE = pl.BlockSpec(memory_space=pl.ANY)
IN_HBM = pl.BlockSpec(memory_space=pltpu.HBM)


def prefix_scratch(count):
    return [pltpu.VMEM((count, HEAD), jnp.bfloat16), pltpu.VMEM((count, 2 * HEAD), jnp.bfloat16)]


def response_call(lengths, order, sent, prefix_kv, blocks):
    responses = lengths.shape[0]
    slot = order.shape[0] // responses
    feat = sent.shape[2]
    span = feat - 2 * HEAD
    return pl.pallas_call(
        response_kernel,
        out_shape=jax.ShapeDtypeStruct((responses, slot, span), jnp.bfloat16),
        in_specs=[SCALARS, WHOLE, IN_HBM, WHOLE] + [WHOLE] * len(blocks),
        out_specs=ANYWHERE,
        scratch_shapes=[pltpu.VMEM((responses * slot, feat), jnp.bfloat16)]
        + prefix_scratch(prefix_kv.shape[0])
        + [
            pltpu.VMEM((responses, slot, span), jnp.bfloat16),
            pltpu.SemaphoreType.DMA((responses, slot // math.gcd(slot, 256))),
            pltpu.SemaphoreType.DMA,
        ],
        compiler_params=pltpu.CompilerParams(vmem_limit_bytes=VMEM_LIMIT),
        cost_estimate=pl.CostEstimate(flops=5 * 10**9, bytes_accessed=4 * 10**6, transcendentals=0),
        name="response_attention",
    )(lengths, order, sent, prefix_kv, *blocks)


def body(prefix_qkv, rollout, arrival_order, resp_len):
    peers = lax.axis_size("prompt")
    ctx_count = lax.axis_size("ctx")
    ctx_index = lax.axis_index("ctx")
    prefix_rows = prefix_qkv[0]
    prefix_len, feat = prefix_rows.shape
    sent = rollout[0, 0]
    assert peers & (peers - 1) == 0

    def after(value, *done):
        return lax.optimization_barrier((value, *done))[0]

    chips = range(1, peers // 2)
    near = [2 * m for m in chips if m.bit_count() == 1]
    far = [2 * m for m in chips if m.bit_count() > 1]
    pairs = [("pair", k) for k in far]
    evens = [("one", k) for k in near]
    odds = [("one", k + 1) for k in near]
    shifts = [("ctx", t) for t in range(1, ctx_count)]
    plan = pairs[:1] + evens[:2] + shifts[:2] + shifts[2:] + odds + evens[2:] + pairs[1:]
    plan += [("one", 1)] if peers > 1 else []
    freed = plan[3:5] + plan[:1] * 2 + plan[1:3] + plan[5:]

    def pick(index, step):
        kind, k = step
        if kind == "pair":
            return lax.dynamic_slice_in_dim(sent, (index ^ k) & -2, 2, 0)
        return lax.dynamic_index_in_dim(sent, index ^ k, 0, keepdims=False)

    own_index = lax.axis_index("prompt")
    core = own_index & 1
    swaps = [step for step in plan if step[0] != "ctx"]
    lead = pick(own_index, swaps[0])
    index, rows, lead = lax.optimization_barrier((own_index, prefix_rows, lead))
    picked = {step: pick(index, step) for step in swaps[1:]}
    picked[swaps[0]] = lead
    prefix_kv = rows[:, feat - 2 * HEAD :]

    got, blocks = {}, {}
    for n, step in enumerate(plan):
        kind, by = step
        if kind == "ctx":
            value, route = prefix_kv, [(j, (j + by) % ctx_count) for j in range(ctx_count)]
        else:
            value, route = picked[step], [(j, j ^ by) for j in range(peers)]
        if n >= 5:
            value = after(value, got[freed[n - 5]])
        got[step] = lax.ppermute(value, "ctx" if kind == "ctx" else "prompt", route)
        if kind == "one":
            blocks[by] = got[step]
    for _, k in pairs:
        came = got["pair", k]
        blocks[k] = lax.dynamic_index_in_dim(came, core, 0, keepdims=False)
        other = lax.dynamic_index_in_dim(came, 1 - core, 0, keepdims=False)
        blocks[k + 1] = lax.ppermute(other, "prompt", [(j, j ^ 1) for j in range(peers)])
    blocks = [blocks[k] for k in range(1, peers)]
    prefix_kv = jnp.concatenate([prefix_kv] + [got[s] for s in shifts], axis=0)

    order = arrival_order[0, 0].reshape(-1, 1)
    starts = (ctx_index - jnp.arange(ctx_count, dtype=jnp.int32)) % ctx_count * prefix_len
    prefix_out = prefix_call(starts, prefix_rows, prefix_kv)
    resp_out = response_call(
        resp_len[0], order, sent, prefix_kv, blocks
    )
    return (prefix_out[None], resp_out[None])


def solution(mesh):
    placed = (
        P("prompt", "ctx", None),
        P("prompt", "ctx", None, None, None),
        P("prompt", "ctx", None),
        P("prompt", "ctx"),
    )
    return jax.shard_map(
        body,
        mesh=mesh,
        in_specs=placed,
        out_specs=(P("prompt", "ctx", None), P("prompt", "ctx", None, None)),
        check_vma=False,
    )
```

```python
import functools
import math

import jax
import jax.numpy as jnp
from jax import lax
from jax.experimental import pallas as pl
from jax.experimental.pallas import tpu as pltpu
from jax.sharding import PartitionSpec as P

HEAD = 128
MASKED_SCORE = -1e30
EXP2_SCALE = HEAD ** (-0.5) * math.log2(math.e)
VMEM_LIMIT = 24 * 1024 * 1024


def mix(a, b):
    return lax.dot_general(a, b, (((1,), (0,)), ((), ())), preferred_element_type=jnp.float32)


def match(a, b):
    return lax.dot_general(a, b, (((1,), (1,)), ((), ())), preferred_element_type=jnp.float32)


def with_ones(values):
    return jnp.concatenate([values, jnp.ones_like(values)], axis=1)


def attend(scores, values):
    top = functools.reduce(jnp.maximum, [jnp.max(s, axis=1, keepdims=True) for s in scores])
    total = None
    for s, v in zip(scores, values):
        weights = jnp.exp2((s - top) * EXP2_SCALE).astype(jnp.bfloat16)
        part = mix(weights, v)
        total = part if total is None else total + part
    return total[:, :HEAD] / total[:, HEAD:]


def prefix_part(starts_ref, rows_ref, pk_ref, pv_ref, out_ref):
    row_count = rows_ref.shape[0]
    heads = rows_ref.shape[1] // HEAD - 2
    row_pos = starts_ref[0] + lax.broadcasted_iota(jnp.int32, (row_count, 1), 0)
    seen = []
    for first in range(0, pk_ref.shape[0], row_count):
        key_pos = starts_ref[first // row_count] + lax.broadcasted_iota(jnp.int32, (1, row_count), 1)
        seen.append(key_pos <= row_pos)
    seen = jnp.concatenate(seen, axis=1)
    seen = jnp.concatenate([seen] * heads, axis=0)
    q = jnp.concatenate([rows_ref[:, h * HEAD : (h + 1) * HEAD] for h in range(heads)], axis=0)
    scores = jnp.where(seen, match(q, pk_ref[...]), MASKED_SCORE)
    result = attend([scores], [pv_ref[...]]).astype(jnp.bfloat16)
    for h in range(heads):
        out_ref[:, h * HEAD : (h + 1) * HEAD] = result[h * row_count : (h + 1) * row_count]


def place(order_ref, arrived, r, slot):
    chosen = lax.broadcasted_iota(jnp.int32, (slot, arrived.shape[0]), 1)
    chosen = chosen == order_ref[r * slot : (r + 1) * slot, :]
    chosen = jnp.where(chosen, 1.0, 0.0).astype(jnp.bfloat16)
    return mix(chosen, arrived).astype(jnp.bfloat16)


def response_part(len_ref, queries, first_head, keys, values, pk_ref, pv_ref, hold_ref, out_ref, sems):
    slot = queries[0].shape[0]
    heads = queries[0].shape[1] // HEAD
    step = math.gcd(slot, 256)
    chunks = slot // step
    causal = lax.broadcasted_iota(jnp.int32, (step, step), 1) <= lax.broadcasted_iota(
        jnp.int32, (step, step), 0
    )
    items = [(r, c, h) for r in range(len(queries)) for c in range(chunks) for h in range(heads)]

    def scored(r, c, h):
        low, high = c * step, (c + 1) * step
        q = queries[r][low:high, h * HEAD : (h + 1) * HEAD]
        scores = [match(q, pk_ref[...])]
        if c:
            scores.append(match(q, keys[r][:low]))
        scores.append(jnp.where(causal, match(q, keys[r][low:high]), MASKED_SCORE))
        return scores

    columns = pl.ds(first_head * HEAD, heads * HEAD)
    copies = []
    ahead = scored(*items[0])
    for n, (r, c, h) in enumerate(items):
        scores = ahead
        if n + 1 < len(items):
            ahead = scored(*items[n + 1])
        low, high = c * step, (c + 1) * step
        value = [pv_ref[...]] + ([values[r][:low]] if c else []) + [values[r][low:high]]
        live = low + lax.broadcasted_iota(jnp.int32, (step, 1), 0) < len_ref[r]
        result = jnp.where(live, attend(scores, value), 0.0)
        hold_ref[r, low:high, h * HEAD : (h + 1) * HEAD] = result.astype(jnp.bfloat16)
        if h == heads - 1:
            copy = pltpu.make_async_copy(
                hold_ref.at[r, pl.ds(low, step)],
                out_ref.at[r, pl.ds(low, step), columns],
                sems.at[r, c],
            )
            copy.start()
            copies.append(copy)
    for copy in copies:
        copy.wait()


def load_prefix(pieces, pk_ref, pv_ref):
    first = 0
    for p in pieces:
        pk_ref[first : first + p.shape[0], :] = p[:, :HEAD]
        pv_ref[first : first + p.shape[0], :] = with_ones(p[:, HEAD:])
        first += p.shape[0]


def prefix_kernel(starts_ref, rows_ref, kv_ref, out_ref, pk_ref, pv_ref):
    load_prefix([kv_ref], pk_ref, pv_ref)
    prefix_part(starts_ref, rows_ref, pk_ref, pv_ref, out_ref)


def prefix_call(starts, rows, kv):
    return pl.pallas_call(
        prefix_kernel,
        out_shape=jax.ShapeDtypeStruct((rows.shape[0], rows.shape[1] - 2 * HEAD), jnp.bfloat16),
        in_specs=[SCALARS, WHOLE, WHOLE],
        out_specs=WHOLE,
        scratch_shapes=prefix_scratch(kv.shape[0]),
        compiler_params=pltpu.CompilerParams(vmem_limit_bytes=VMEM_LIMIT),
        cost_estimate=pl.CostEstimate(flops=10**9, bytes_accessed=10**6, transcendentals=0),
        name="prefix_attention",
    )(starts, rows, kv)


def response_kernel(len_ref, order_ref, sent_ref, prefix_ref, *refs):
    blocks = refs[:-7]
    out_ref, arrived_ref, pk_ref, pv_ref, hold_ref, sems, own_sem = refs[-7:]
    responses, slot, span = hold_ref.shape
    index = lax.axis_index("prompt")
    rows_peer = sent_ref.shape[1]
    first = pl.multiple_of(index * rows_peer, rows_peer)
    own = pltpu.make_async_copy(
        sent_ref.at[index], arrived_ref.at[pl.ds(first, rows_peer)], own_sem
    )
    own.start()
    load_prefix([prefix_ref], pk_ref, pv_ref)
    for k, b in enumerate(blocks, 1):
        first = pl.multiple_of((index ^ k) * rows_peer, rows_peer)
        arrived_ref[pl.ds(first, rows_peer), :] = b[...]
    own.wait()
    placed = [place(order_ref, arrived_ref[...], r, slot) for r in range(responses)]
    response_part(
        len_ref,
        [p[:, :span] for p in placed],
        0,
        [p[:, span : span + HEAD] for p in placed],
        [with_ones(p[:, span + HEAD :]) for p in placed],
        pk_ref,
        pv_ref,
        hold_ref,
        out_ref,
        sems,
    )


WHOLE = pl.BlockSpec(memory_space=pltpu.VMEM)
SCALARS = pl.BlockSpec(memory_space=pltpu.SMEM)
ANYWHERE = pl.BlockSpec(memory_space=pl.ANY)
IN_HBM = pl.BlockSpec(memory_space=pltpu.HBM)


def prefix_scratch(count):
    return [pltpu.VMEM((count, HEAD), jnp.bfloat16), pltpu.VMEM((count, 2 * HEAD), jnp.bfloat16)]


def response_call(lengths, order, sent, prefix_kv, blocks):
    responses = lengths.shape[0]
    slot = order.shape[0] // responses
    feat = sent.shape[2]
    span = feat - 2 * HEAD
    return pl.pallas_call(
        response_kernel,
        out_shape=jax.ShapeDtypeStruct((responses, slot, span), jnp.bfloat16),
        in_specs=[SCALARS, WHOLE, IN_HBM, WHOLE] + [WHOLE] * len(blocks),
        out_specs=ANYWHERE,
        scratch_shapes=[pltpu.VMEM((responses * slot, feat), jnp.bfloat16)]
        + prefix_scratch(prefix_kv.shape[0])
        + [
            pltpu.VMEM((responses, slot, span), jnp.bfloat16),
            pltpu.SemaphoreType.DMA((responses, slot // math.gcd(slot, 256))),
            pltpu.SemaphoreType.DMA,
        ],
        compiler_params=pltpu.CompilerParams(vmem_limit_bytes=VMEM_LIMIT),
        cost_estimate=pl.CostEstimate(flops=5 * 10**9, bytes_accessed=4 * 10**6, transcendentals=0),
        name="response_attention",
    )(lengths, order, sent, prefix_kv, *blocks)


def body(prefix_qkv, rollout, arrival_order, resp_len):
    peers = lax.axis_size("prompt")
    ctx_count = lax.axis_size("ctx")
    ctx_index = lax.axis_index("ctx")
    prefix_rows = prefix_qkv[0]
    prefix_len, feat = prefix_rows.shape
    sent = rollout[0, 0]
    assert peers & (peers - 1) == 0

    def after(value, *done):
        return lax.optimization_barrier((value, *done))[0]

    chips = range(1, peers // 2)
    near = [2 * m for m in chips if m.bit_count() == 1]
    far = [2 * m for m in chips if m.bit_count() > 1]
    pairs = [("pair", k) for k in far]
    evens = [("one", k) for k in near]
    odds = [("one", k + 1) for k in near]
    turns = sorted(range(1, ctx_count), key=lambda t: -min(t, ctx_count - t))
    shifts = [("ctx", t) for t in turns]
    plan = pairs[:1] + evens[:2] + shifts[:2] + shifts[2:] + odds + evens[2:] + pairs[1:]
    plan += [("one", 1)] if peers > 1 else []
    freed = plan[3:5] + plan[:1] * 2 + plan[1:3] + plan[5:]

    def pick(index, step):
        kind, k = step
        if kind == "pair":
            return lax.dynamic_slice_in_dim(sent, (index ^ k) & -2, 2, 0)
        return lax.dynamic_index_in_dim(sent, index ^ k, 0, keepdims=False)

    own_index = lax.axis_index("prompt")
    core = own_index & 1
    swaps = [step for step in plan if step[0] != "ctx"]
    lead = pick(own_index, swaps[0])
    index, rows, lead = lax.optimization_barrier((own_index, prefix_rows, lead))
    picked = {step: pick(index, step) for step in swaps[1:]}
    picked[swaps[0]] = lead
    prefix_kv = rows[:, feat - 2 * HEAD :]

    got, blocks = {}, {}
    for n, step in enumerate(plan):
        kind, by = step
        if kind == "ctx":
            value, route = prefix_kv, [(j, (j + by) % ctx_count) for j in range(ctx_count)]
        else:
            value, route = picked[step], [(j, j ^ by) for j in range(peers)]
        if n >= 5:
            value = after(value, got[freed[n - 5]])
        got[step] = lax.ppermute(value, "ctx" if kind == "ctx" else "prompt", route)
        if kind == "one":
            blocks[by] = got[step]
    for _, k in pairs:
        came = got["pair", k]
        blocks[k] = lax.dynamic_index_in_dim(came, core, 0, keepdims=False)
        other = lax.dynamic_index_in_dim(came, 1 - core, 0, keepdims=False)
        blocks[k + 1] = lax.ppermute(other, "prompt", [(j, j ^ 1) for j in range(peers)])
    blocks = [blocks[k] for k in range(1, peers)]
    prefix_kv = jnp.concatenate([prefix_kv] + [got["ctx", t] for t in range(1, ctx_count)], axis=0)

    order = arrival_order[0, 0].reshape(-1, 1)
    starts = (ctx_index - jnp.arange(ctx_count, dtype=jnp.int32)) % ctx_count * prefix_len
    prefix_out = prefix_call(starts, prefix_rows, prefix_kv)
    resp_out = response_call(
        resp_len[0], order, sent, prefix_kv, blocks
    )
    return (prefix_out[None], resp_out[None])


def solution(mesh):
    placed = (
        P("prompt", "ctx", None),
        P("prompt", "ctx", None, None, None),
        P("prompt", "ctx", None),
        P("prompt", "ctx"),
    )
    return jax.shard_map(
        body,
        mesh=mesh,
        in_specs=placed,
        out_specs=(P("prompt", "ctx", None), P("prompt", "ctx", None, None)),
        check_vma=False,
    )
```

```python
import functools
import math

import jax
import jax.numpy as jnp
from jax import lax
from jax.experimental import pallas as pl
from jax.experimental.pallas import tpu as pltpu
from jax.sharding import PartitionSpec as P

HEAD = 128
MASKED_SCORE = -1e30
EXP2_SCALE = HEAD ** (-0.5) * math.log2(math.e)
VMEM_LIMIT = 24 * 1024 * 1024


def mix(a, b):
    return lax.dot_general(a, b, (((1,), (0,)), ((), ())), preferred_element_type=jnp.float32)


def match(a, b):
    return lax.dot_general(a, b, (((1,), (1,)), ((), ())), preferred_element_type=jnp.float32)


def with_ones(values):
    return jnp.concatenate([values, jnp.ones_like(values)], axis=1)


def upright(values):
    ones = jnp.ones((16, values.shape[0]), jnp.bfloat16)
    return jnp.concatenate([values.T, ones], axis=0)


def scaled_keys(keys):
    scaled = keys.astype(jnp.float32) * EXP2_SCALE
    high = scaled.astype(jnp.bfloat16)
    low = (scaled - high.astype(jnp.float32)).astype(jnp.bfloat16)
    return jnp.concatenate([high, low], axis=1)


def twice(queries):
    return jnp.concatenate([queries, queries], axis=1)


def attend(scores, values):
    top = functools.reduce(jnp.maximum, [jnp.max(s, axis=1, keepdims=True) for s in scores])
    total = None
    for s, v in zip(scores, values):
        weights = jnp.exp2(s - top).astype(jnp.bfloat16)
        part = mix(weights, v)
        total = part if total is None else total + part
    return total[:, :HEAD] / total[:, HEAD:]


def prefix_part(starts_ref, rows_ref, pk_ref, pv_ref, out_ref):
    row_count = rows_ref.shape[0]
    heads = rows_ref.shape[1] // HEAD - 2
    row_pos = starts_ref[0] + lax.broadcasted_iota(jnp.int32, (row_count, 1), 0)
    seen = []
    for first in range(0, pk_ref.shape[0], row_count):
        key_pos = starts_ref[first // row_count] + lax.broadcasted_iota(jnp.int32, (1, row_count), 1)
        seen.append(key_pos <= row_pos)
    seen = jnp.concatenate(seen, axis=1)
    seen = jnp.concatenate([seen] * heads, axis=0)
    q = jnp.concatenate([rows_ref[:, h * HEAD : (h + 1) * HEAD] for h in range(heads)], axis=0)
    scores = jnp.where(seen, match(twice(q), pk_ref[...]), MASKED_SCORE)
    result = attend([scores], [pv_ref[...]]).astype(jnp.bfloat16)
    for h in range(heads):
        out_ref[:, h * HEAD : (h + 1) * HEAD] = result[h * row_count : (h + 1) * row_count]


def place(order_ref, arrived, r, slot):
    chosen = lax.broadcasted_iota(jnp.int32, (slot, arrived.shape[0]), 1)
    chosen = chosen == order_ref[r * slot : (r + 1) * slot, :]
    chosen = jnp.where(chosen, 1.0, 0.0).astype(jnp.bfloat16)
    return mix(chosen, arrived).astype(jnp.bfloat16)


def response_part(len_ref, queries, keys, values, pk_ref, pv_ref, hold_ref, out_ref, sems):
    slot = queries[0].shape[0]
    heads = queries[0].shape[1] // HEAD
    step = math.gcd(slot, 256)
    chunks = slot // step
    causal = lax.broadcasted_iota(jnp.int32, (step, step), 0) <= lax.broadcasted_iota(
        jnp.int32, (step, step), 1
    )
    items = [(r, c, h) for r in range(len(queries)) for c in range(chunks) for h in range(heads)]
    prefix_values = upright(pv_ref[:, :HEAD])
    own_values = [upright(v) for v in values]

    def scored(r, c, h):
        low, high = c * step, (c + 1) * step
        q = twice(queries[r][low:high, h * HEAD : (h + 1) * HEAD])
        scores = [match(pk_ref[...], q)]
        if c:
            scores.append(match(keys[r][:low], q))
        scores.append(jnp.where(causal, match(keys[r][low:high], q), MASKED_SCORE))
        return scores

    def weighed(scores):
        top = functools.reduce(jnp.maximum, [jnp.max(s, axis=0, keepdims=True) for s in scores])
        return [jnp.exp2(s - top).astype(jnp.bfloat16) for s in scores]

    def summed(weights, values, live):
        total = functools.reduce(jnp.add, [mix(v, w) for w, v in zip(weights, values)])
        share = jnp.where(live, 1.0 / total[HEAD : HEAD + 1], 0.0)
        return (total[:HEAD] * share).astype(jnp.bfloat16).T

    copies = []
    ready = weighed(scored(*items[0]))
    ahead = scored(*items[1]) if len(items) > 1 else None
    for n, (r, c, h) in enumerate(items):
        weights, scores = ready, ahead
        if n + 2 < len(items):
            ahead = scored(*items[n + 2])
        if n + 1 < len(items):
            ready = weighed(scores)
        low, high = c * step, (c + 1) * step
        value = [prefix_values]
        if c:
            value.append(own_values[r][:, :low])
        value.append(own_values[r][:, low:high])
        live = low + lax.broadcasted_iota(jnp.int32, (1, step), 1) < len_ref[r]
        result = summed(weights, value, live).astype(jnp.bfloat16)
        hold_ref[r, low:high, h * HEAD : (h + 1) * HEAD] = result
        if h == heads - 1:
            copy = pltpu.make_async_copy(
                hold_ref.at[r, pl.ds(low, step)], out_ref.at[r, pl.ds(low, step)], sems.at[r, c]
            )
            copy.start()
            copies.append(copy)
    for copy in copies:
        copy.wait()


def load_prefix(pieces, pk_ref, pv_ref):
    first = 0
    for p in pieces:
        pk_ref[first : first + p.shape[0], :] = scaled_keys(p[:, :HEAD])
        pv_ref[first : first + p.shape[0], :] = with_ones(p[:, HEAD:])
        first += p.shape[0]


def prefix_kernel(starts_ref, rows_ref, kv_ref, out_ref, pk_ref, pv_ref):
    load_prefix([kv_ref], pk_ref, pv_ref)
    prefix_part(starts_ref, rows_ref, pk_ref, pv_ref, out_ref)


def prefix_call(starts, rows, kv):
    return pl.pallas_call(
        prefix_kernel,
        out_shape=jax.ShapeDtypeStruct((rows.shape[0], rows.shape[1] - 2 * HEAD), jnp.bfloat16),
        in_specs=[SCALARS, WHOLE, WHOLE],
        out_specs=WHOLE,
        scratch_shapes=prefix_scratch(kv.shape[0]),
        compiler_params=pltpu.CompilerParams(vmem_limit_bytes=VMEM_LIMIT),
        cost_estimate=pl.CostEstimate(flops=10**9, bytes_accessed=10**6, transcendentals=0),
        name="prefix_attention",
    )(starts, rows, kv)


def response_kernel(len_ref, order_ref, sent_ref, prefix_ref, *refs):
    blocks = refs[:-7]
    out_ref, arrived_ref, pk_ref, pv_ref, hold_ref, sems, own_sem = refs[-7:]
    responses, slot, span = hold_ref.shape
    index = lax.axis_index("prompt")
    rows_peer = sent_ref.shape[1]
    first = pl.multiple_of(index * rows_peer, rows_peer)
    own = pltpu.make_async_copy(
        sent_ref.at[index], arrived_ref.at[pl.ds(first, rows_peer)], own_sem
    )
    own.start()
    load_prefix([prefix_ref], pk_ref, pv_ref)
    for k, b in enumerate(blocks, 1):
        first = pl.multiple_of((index ^ k) * rows_peer, rows_peer)
        arrived_ref[pl.ds(first, rows_peer), :] = b[...]
    own.wait()
    placed = [place(order_ref, arrived_ref[...], r, slot) for r in range(responses)]
    response_part(
        len_ref,
        [p[:, :span] for p in placed],
        [scaled_keys(p[:, span : span + HEAD]) for p in placed],
        [p[:, span + HEAD :] for p in placed],
        pk_ref,
        pv_ref,
        hold_ref,
        out_ref,
        sems,
    )


WHOLE = pl.BlockSpec(memory_space=pltpu.VMEM)
SCALARS = pl.BlockSpec(memory_space=pltpu.SMEM)
ANYWHERE = pl.BlockSpec(memory_space=pl.ANY)
IN_HBM = pl.BlockSpec(memory_space=pltpu.HBM)


def prefix_scratch(count):
    return [pltpu.VMEM((count, 2 * HEAD), jnp.bfloat16)] * 2


def response_call(lengths, order, sent, prefix_kv, blocks):
    responses = lengths.shape[0]
    slot = order.shape[0] // responses
    feat = sent.shape[2]
    span = feat - 2 * HEAD
    return pl.pallas_call(
        response_kernel,
        out_shape=jax.ShapeDtypeStruct((responses, slot, span), jnp.bfloat16),
        in_specs=[SCALARS, WHOLE, IN_HBM, WHOLE] + [WHOLE] * len(blocks),
        out_specs=ANYWHERE,
        scratch_shapes=[pltpu.VMEM((responses * slot, feat), jnp.bfloat16)]
        + prefix_scratch(prefix_kv.shape[0])
        + [
            pltpu.VMEM((responses, slot, span), jnp.bfloat16),
            pltpu.SemaphoreType.DMA((responses, slot // math.gcd(slot, 256))),
            pltpu.SemaphoreType.DMA,
        ],
        compiler_params=pltpu.CompilerParams(vmem_limit_bytes=VMEM_LIMIT),
        cost_estimate=pl.CostEstimate(flops=5 * 10**9, bytes_accessed=4 * 10**6, transcendentals=0),
        name="response_attention",
    )(lengths, order, sent, prefix_kv, *blocks)


def body(prefix_qkv, rollout, arrival_order, resp_len):
    peers = lax.axis_size("prompt")
    ctx_count = lax.axis_size("ctx")
    ctx_index = lax.axis_index("ctx")
    prefix_rows = prefix_qkv[0]
    prefix_len, feat = prefix_rows.shape
    sent = rollout[0, 0]
    assert peers & (peers - 1) == 0

    def after(value, *done):
        return lax.optimization_barrier((value, *done))[0]

    chips = range(1, peers // 2)
    near = [2 * m for m in chips if m.bit_count() == 1]
    far = [2 * m for m in chips if m.bit_count() > 1]
    pairs = [("pair", k) for k in far]
    evens = [("one", k) for k in near]
    odds = [("one", k + 1) for k in near]
    turns = sorted(range(1, ctx_count), key=lambda t: -min(t, ctx_count - t))
    shifts = [("ctx", t) for t in turns]
    plan = pairs[:1] + evens[:2] + shifts[:2] + shifts[2:] + odds + evens[2:] + pairs[1:]
    plan += [("one", 1)] if peers > 1 else []
    freed = plan[3:5] + plan[:1] * 2 + plan[1:3] + plan[5:]

    def pick(index, step):
        kind, k = step
        if kind == "pair":
            return lax.dynamic_slice_in_dim(sent, (index ^ k) & -2, 2, 0)
        return lax.dynamic_index_in_dim(sent, index ^ k, 0, keepdims=False)

    own_index = lax.axis_index("prompt")
    core = own_index & 1
    swaps = [step for step in plan if step[0] != "ctx"]
    lead = pick(own_index, swaps[0])
    index, rows, lead = lax.optimization_barrier((own_index, prefix_rows, lead))
    picked = {step: pick(index, step) for step in swaps[1:]}
    picked[swaps[0]] = lead
    prefix_kv = rows[:, feat - 2 * HEAD :]

    got, blocks = {}, {}
    for n, step in enumerate(plan):
        kind, by = step
        if kind == "ctx":
            value, route = prefix_kv, [(j, (j + by) % ctx_count) for j in range(ctx_count)]
        else:
            value, route = picked[step], [(j, j ^ by) for j in range(peers)]
        if n >= 5:
            value = after(value, got[freed[n - 5]])
        got[step] = lax.ppermute(value, "ctx" if kind == "ctx" else "prompt", route)
        if kind == "one":
            blocks[by] = got[step]
    for _, k in pairs:
        came = got["pair", k]
        blocks[k] = lax.dynamic_index_in_dim(came, core, 0, keepdims=False)
        other = lax.dynamic_index_in_dim(came, 1 - core, 0, keepdims=False)
        blocks[k + 1] = lax.ppermute(other, "prompt", [(j, j ^ 1) for j in range(peers)])
    blocks = [blocks[k] for k in range(1, peers)]
    prefix_kv = jnp.concatenate([prefix_kv] + [got["ctx", t] for t in range(1, ctx_count)], axis=0)

    order = arrival_order[0, 0].reshape(-1, 1)
    starts = (ctx_index - jnp.arange(ctx_count, dtype=jnp.int32)) % ctx_count * prefix_len
    prefix_out = prefix_call(starts, prefix_rows, prefix_kv)
    resp_out = response_call(
        resp_len[0], order, sent, prefix_kv, blocks
    )
    return (prefix_out[None], resp_out[None])


def solution(mesh):
    placed = (
        P("prompt", "ctx", None),
        P("prompt", "ctx", None, None, None),
        P("prompt", "ctx", None),
        P("prompt", "ctx"),
    )
    return jax.shard_map(
        body,
        mesh=mesh,
        in_specs=placed,
        out_specs=(P("prompt", "ctx", None), P("prompt", "ctx", None, None)),
        check_vma=False,
    )
```

```python
import functools
import math

import jax
import jax.numpy as jnp
from jax import lax
from jax.experimental import pallas as pl
from jax.experimental.pallas import tpu as pltpu
from jax.sharding import PartitionSpec as P

HEAD = 128
MASKED_SCORE = -1e30
EXP2_SCALE = HEAD ** (-0.5) * math.log2(math.e)
VMEM_LIMIT = 24 * 1024 * 1024


def mix(a, b):
    return lax.dot_general(a, b, (((1,), (0,)), ((), ())), preferred_element_type=jnp.float32)


def match(a, b):
    return lax.dot_general(a, b, (((1,), (1,)), ((), ())), preferred_element_type=jnp.float32)


def with_ones(values):
    return jnp.concatenate([values, jnp.ones_like(values)], axis=1)


def upright(values):
    ones = jnp.ones((16, values.shape[0]), jnp.bfloat16)
    return jnp.concatenate([values.T, ones], axis=0)


def scaled_keys(keys):
    scaled = keys.astype(jnp.float32) * EXP2_SCALE
    high = scaled.astype(jnp.bfloat16)
    low = (scaled - high.astype(jnp.float32)).astype(jnp.bfloat16)
    return jnp.concatenate([high, low], axis=1)


def twice(queries):
    return jnp.concatenate([queries, queries], axis=1)


def attend(scores, values):
    top = functools.reduce(jnp.maximum, [jnp.max(s, axis=1, keepdims=True) for s in scores])
    total = None
    for s, v in zip(scores, values):
        weights = jnp.exp2(s - top).astype(jnp.bfloat16)
        part = mix(weights, v)
        total = part if total is None else total + part
    return total[:, :HEAD] / total[:, HEAD:]


def prefix_part(starts_ref, rows_ref, pk_ref, pv_ref, out_ref):
    row_count = rows_ref.shape[0]
    heads = rows_ref.shape[1] // HEAD - 2
    row_pos = starts_ref[0] + lax.broadcasted_iota(jnp.int32, (row_count, 1), 0)
    seen = []
    for first in range(0, pk_ref.shape[0], row_count):
        key_pos = starts_ref[first // row_count] + lax.broadcasted_iota(jnp.int32, (1, row_count), 1)
        seen.append(key_pos <= row_pos)
    seen = jnp.concatenate(seen, axis=1)
    seen = jnp.concatenate([seen] * heads, axis=0)
    q = jnp.concatenate([rows_ref[:, h * HEAD : (h + 1) * HEAD] for h in range(heads)], axis=0)
    scores = jnp.where(seen, match(twice(q), pk_ref[...]), MASKED_SCORE)
    result = attend([scores], [pv_ref[...]]).astype(jnp.bfloat16)
    for h in range(heads):
        out_ref[:, h * HEAD : (h + 1) * HEAD] = result[h * row_count : (h + 1) * row_count]


def place(order_ref, arrived, r, slot):
    chosen = lax.broadcasted_iota(jnp.int32, (slot, arrived.shape[0]), 1)
    chosen = chosen == order_ref[r * slot : (r + 1) * slot, :]
    chosen = jnp.where(chosen, 1.0, 0.0).astype(jnp.bfloat16)
    return mix(chosen, arrived).astype(jnp.bfloat16)


def response_part(len_ref, queries, keys, values, pk_ref, pv_ref, hold_ref, out_ref, sems):
    slot = queries[0].shape[0]
    heads = queries[0].shape[1] // HEAD
    step = math.gcd(slot, 256)
    chunks = slot // step
    causal = lax.broadcasted_iota(jnp.int32, (step, step), 0) <= lax.broadcasted_iota(
        jnp.int32, (step, step), 1
    )
    items = [(r, c, h) for r in range(len(queries)) for c in range(chunks) for h in range(heads)]
    prefix_values = upright(pv_ref[:, :HEAD])
    all_values = [jnp.concatenate([prefix_values, upright(v)], axis=1) for v in values]

    def scored(r, c, h):
        low, high = c * step, (c + 1) * step
        q = twice(queries[r][low:high, h * HEAD : (h + 1) * HEAD])
        scores = [match(pk_ref[...], q)]
        if c:
            scores.append(match(keys[r][:low], q))
        scores.append(jnp.where(causal, match(keys[r][low:high], q), MASKED_SCORE))
        return scores

    def weighed(scores):
        top = functools.reduce(jnp.maximum, [jnp.max(s, axis=0, keepdims=True) for s in scores])
        return [jnp.exp2(s - top).astype(jnp.bfloat16) for s in scores]

    def summed(weights, values, live):
        total = mix(values, jnp.concatenate(weights, axis=0))
        share = jnp.where(live, 1.0 / total[HEAD : HEAD + 1], 0.0)
        return (total[:HEAD] * share).astype(jnp.bfloat16).T

    copies = []
    ready = weighed(scored(*items[0]))
    ahead = scored(*items[1]) if len(items) > 1 else None
    for n, (r, c, h) in enumerate(items):
        weights, scores = ready, ahead
        if n + 2 < len(items):
            ahead = scored(*items[n + 2])
        if n + 1 < len(items):
            ready = weighed(scores)
        low, high = c * step, (c + 1) * step
        value = all_values[r][:, : prefix_values.shape[1] + high]
        live = low + lax.broadcasted_iota(jnp.int32, (1, step), 1) < len_ref[r]
        result = summed(weights, value, live).astype(jnp.bfloat16)
        hold_ref[r, low:high, h * HEAD : (h + 1) * HEAD] = result
        if h == heads - 1:
            copy = pltpu.make_async_copy(
                hold_ref.at[r, pl.ds(low, step)], out_ref.at[r, pl.ds(low, step)], sems.at[r, c]
            )
            copy.start()
            copies.append(copy)
    for copy in copies:
        copy.wait()


def load_prefix(pieces, pk_ref, pv_ref):
    first = 0
    for p in pieces:
        pk_ref[first : first + p.shape[0], :] = scaled_keys(p[:, :HEAD])
        pv_ref[first : first + p.shape[0], :] = with_ones(p[:, HEAD:])
        first += p.shape[0]


def prefix_kernel(starts_ref, rows_ref, kv_ref, out_ref, pk_ref, pv_ref):
    load_prefix([kv_ref], pk_ref, pv_ref)
    prefix_part(starts_ref, rows_ref, pk_ref, pv_ref, out_ref)


def prefix_call(starts, rows, kv):
    return pl.pallas_call(
        prefix_kernel,
        out_shape=jax.ShapeDtypeStruct((rows.shape[0], rows.shape[1] - 2 * HEAD), jnp.bfloat16),
        in_specs=[SCALARS, WHOLE, WHOLE],
        out_specs=WHOLE,
        scratch_shapes=prefix_scratch(kv.shape[0]),
        compiler_params=pltpu.CompilerParams(vmem_limit_bytes=VMEM_LIMIT),
        cost_estimate=pl.CostEstimate(flops=10**9, bytes_accessed=10**6, transcendentals=0),
        name="prefix_attention",
    )(starts, rows, kv)


def response_kernel(len_ref, order_ref, sent_ref, prefix_ref, *refs):
    blocks = refs[:-7]
    out_ref, arrived_ref, pk_ref, pv_ref, hold_ref, sems, own_sem = refs[-7:]
    responses, slot, span = hold_ref.shape
    index = lax.axis_index("prompt")
    rows_peer = sent_ref.shape[1]
    first = pl.multiple_of(index * rows_peer, rows_peer)
    own = pltpu.make_async_copy(
        sent_ref.at[index], arrived_ref.at[pl.ds(first, rows_peer)], own_sem
    )
    own.start()
    load_prefix([prefix_ref], pk_ref, pv_ref)
    for k, b in enumerate(blocks, 1):
        first = pl.multiple_of((index ^ k) * rows_peer, rows_peer)
        arrived_ref[pl.ds(first, rows_peer), :] = b[...]
    own.wait()
    placed = [place(order_ref, arrived_ref[...], r, slot) for r in range(responses)]
    response_part(
        len_ref,
        [p[:, :span] for p in placed],
        [scaled_keys(p[:, span : span + HEAD]) for p in placed],
        [p[:, span + HEAD :] for p in placed],
        pk_ref,
        pv_ref,
        hold_ref,
        out_ref,
        sems,
    )


WHOLE = pl.BlockSpec(memory_space=pltpu.VMEM)
SCALARS = pl.BlockSpec(memory_space=pltpu.SMEM)
ANYWHERE = pl.BlockSpec(memory_space=pl.ANY)
IN_HBM = pl.BlockSpec(memory_space=pltpu.HBM)


def prefix_scratch(count):
    return [pltpu.VMEM((count, 2 * HEAD), jnp.bfloat16)] * 2


def response_call(lengths, order, sent, prefix_kv, blocks):
    responses = lengths.shape[0]
    slot = order.shape[0] // responses
    feat = sent.shape[2]
    span = feat - 2 * HEAD
    return pl.pallas_call(
        response_kernel,
        out_shape=jax.ShapeDtypeStruct((responses, slot, span), jnp.bfloat16),
        in_specs=[SCALARS, WHOLE, IN_HBM, WHOLE] + [WHOLE] * len(blocks),
        out_specs=ANYWHERE,
        scratch_shapes=[pltpu.VMEM((responses * slot, feat), jnp.bfloat16)]
        + prefix_scratch(prefix_kv.shape[0])
        + [
            pltpu.VMEM((responses, slot, span), jnp.bfloat16),
            pltpu.SemaphoreType.DMA((responses, slot // math.gcd(slot, 256))),
            pltpu.SemaphoreType.DMA,
        ],
        compiler_params=pltpu.CompilerParams(vmem_limit_bytes=VMEM_LIMIT),
        cost_estimate=pl.CostEstimate(flops=5 * 10**9, bytes_accessed=4 * 10**6, transcendentals=0),
        name="response_attention",
    )(lengths, order, sent, prefix_kv, *blocks)


def body(prefix_qkv, rollout, arrival_order, resp_len):
    peers = lax.axis_size("prompt")
    ctx_count = lax.axis_size("ctx")
    ctx_index = lax.axis_index("ctx")
    prefix_rows = prefix_qkv[0]
    prefix_len, feat = prefix_rows.shape
    sent = rollout[0, 0]
    assert peers & (peers - 1) == 0

    def after(value, *done):
        return lax.optimization_barrier((value, *done))[0]

    chips = range(1, peers // 2)
    near = [2 * m for m in chips if m.bit_count() == 1]
    far = [2 * m for m in chips if m.bit_count() > 1]
    pairs = [("pair", k) for k in far]
    evens = [("one", k) for k in near]
    odds = [("one", k + 1) for k in near]
    turns = sorted(range(1, ctx_count), key=lambda t: -min(t, ctx_count - t))
    shifts = [("ctx", t) for t in turns]
    plan = pairs[:1] + evens[:2] + shifts[:2] + shifts[2:] + odds + evens[2:] + pairs[1:]
    plan += [("one", 1)] if peers > 1 else []
    freed = plan[3:5] + plan[:1] * 2 + plan[1:3] + plan[5:]

    def pick(index, step):
        kind, k = step
        if kind == "pair":
            return lax.dynamic_slice_in_dim(sent, (index ^ k) & -2, 2, 0)
        return lax.dynamic_index_in_dim(sent, index ^ k, 0, keepdims=False)

    own_index = lax.axis_index("prompt")
    core = own_index & 1
    swaps = [step for step in plan if step[0] != "ctx"]
    lead = pick(own_index, swaps[0])
    index, rows, lead = lax.optimization_barrier((own_index, prefix_rows, lead))
    picked = {step: pick(index, step) for step in swaps[1:]}
    picked[swaps[0]] = lead
    prefix_kv = rows[:, feat - 2 * HEAD :]

    got, blocks = {}, {}
    for n, step in enumerate(plan):
        kind, by = step
        if kind == "ctx":
            value, route = prefix_kv, [(j, (j + by) % ctx_count) for j in range(ctx_count)]
        else:
            value, route = picked[step], [(j, j ^ by) for j in range(peers)]
        if n >= 5:
            value = after(value, got[freed[n - 5]])
        got[step] = lax.ppermute(value, "ctx" if kind == "ctx" else "prompt", route)
        if kind == "one":
            blocks[by] = got[step]
    for _, k in pairs:
        came = got["pair", k]
        blocks[k] = lax.dynamic_index_in_dim(came, core, 0, keepdims=False)
        other = lax.dynamic_index_in_dim(came, 1 - core, 0, keepdims=False)
        blocks[k + 1] = lax.ppermute(other, "prompt", [(j, j ^ 1) for j in range(peers)])
    blocks = [blocks[k] for k in range(1, peers)]
    prefix_kv = jnp.concatenate([prefix_kv] + [got["ctx", t] for t in range(1, ctx_count)], axis=0)

    order = arrival_order[0, 0].reshape(-1, 1)
    starts = (ctx_index - jnp.arange(ctx_count, dtype=jnp.int32)) % ctx_count * prefix_len
    prefix_out = prefix_call(starts, prefix_rows, prefix_kv)
    resp_out = response_call(
        resp_len[0], order, sent, prefix_kv, blocks
    )
    return (prefix_out[None], resp_out[None])


def solution(mesh):
    placed = (
        P("prompt", "ctx", None),
        P("prompt", "ctx", None, None, None),
        P("prompt", "ctx", None),
        P("prompt", "ctx"),
    )
    return jax.shard_map(
        body,
        mesh=mesh,
        in_specs=placed,
        out_specs=(P("prompt", "ctx", None), P("prompt", "ctx", None, None)),
        check_vma=False,
    )
```

```python
import functools
import math

import jax
import jax.numpy as jnp
from jax import lax
from jax.experimental import pallas as pl
from jax.experimental.pallas import tpu as pltpu
from jax.sharding import PartitionSpec as P

HEAD = 128
MASKED_SCORE = -1e30
EXP2_SCALE = HEAD ** (-0.5) * math.log2(math.e)
VMEM_LIMIT = 24 * 1024 * 1024


def mix(a, b):
    return lax.dot_general(a, b, (((1,), (0,)), ((), ())), preferred_element_type=jnp.float32)


def match(a, b):
    return lax.dot_general(a, b, (((1,), (1,)), ((), ())), preferred_element_type=jnp.float32)


def with_ones(values):
    return jnp.concatenate([values, jnp.ones_like(values)], axis=1)


def upright(values):
    ones = jnp.ones((16, values.shape[0]), jnp.bfloat16)
    return jnp.concatenate([values.T, ones], axis=0)


def scaled_keys(keys):
    scaled = keys.astype(jnp.float32) * EXP2_SCALE
    high = scaled.astype(jnp.bfloat16)
    low = (scaled - high.astype(jnp.float32)).astype(jnp.bfloat16)
    return jnp.concatenate([high, low], axis=1)


def twice(queries):
    return jnp.concatenate([queries, queries], axis=1)


def attend(scores, values):
    top = functools.reduce(jnp.maximum, [jnp.max(s, axis=1, keepdims=True) for s in scores])
    total = None
    for s, v in zip(scores, values):
        weights = jnp.exp2(s - top).astype(jnp.bfloat16)
        part = mix(weights, v)
        total = part if total is None else total + part
    return total[:, :HEAD] / total[:, HEAD:]


def prefix_part(starts_ref, rows_ref, pk_ref, pv_ref, out_ref):
    row_count = rows_ref.shape[0]
    heads = rows_ref.shape[1] // HEAD - 2
    row_pos = starts_ref[0] + lax.broadcasted_iota(jnp.int32, (row_count, 1), 0)
    seen = []
    for first in range(0, pk_ref.shape[0], row_count):
        key_pos = starts_ref[first // row_count] + lax.broadcasted_iota(jnp.int32, (1, row_count), 1)
        seen.append(key_pos <= row_pos)
    seen = jnp.concatenate(seen, axis=1)
    seen = jnp.concatenate([seen] * heads, axis=0)
    q = jnp.concatenate([rows_ref[:, h * HEAD : (h + 1) * HEAD] for h in range(heads)], axis=0)
    scores = jnp.where(seen, match(twice(q), pk_ref[...]), MASKED_SCORE)
    result = attend([scores], [pv_ref[...]]).astype(jnp.bfloat16)
    for h in range(heads):
        out_ref[:, h * HEAD : (h + 1) * HEAD] = result[h * row_count : (h + 1) * row_count]


def place(order_ref, arrived, r, slot):
    chosen = lax.broadcasted_iota(jnp.int32, (slot, arrived.shape[0]), 1)
    chosen = chosen == order_ref[r * slot : (r + 1) * slot, :]
    chosen = jnp.where(chosen, 1.0, 0.0).astype(jnp.bfloat16)
    return mix(chosen, arrived).astype(jnp.bfloat16)


def response_part(len_ref, queries, keys, values, pk_ref, pv_ref, hold_ref, out_ref, sems):
    slot = queries[0].shape[0]
    heads = queries[0].shape[1] // HEAD
    step = math.gcd(slot, 256)
    chunks = slot // step
    causal = lax.broadcasted_iota(jnp.int32, (step, step), 0) <= lax.broadcasted_iota(
        jnp.int32, (step, step), 1
    )
    items = [(r, c, h) for r in range(len(queries)) for c in reversed(range(chunks)) for h in range(heads)]
    prefix_values = upright(pv_ref[:, :HEAD])
    all_values = [jnp.concatenate([prefix_values, upright(v)], axis=1) for v in values]

    def scored(r, c, h):
        low, high = c * step, (c + 1) * step
        q = twice(queries[r][low:high, h * HEAD : (h + 1) * HEAD])
        scores = [match(pk_ref[...], q)]
        if c:
            scores.append(match(keys[r][:low], q))
        scores.append(jnp.where(causal, match(keys[r][low:high], q), MASKED_SCORE))
        return scores

    def weighed(scores):
        top = functools.reduce(jnp.maximum, [jnp.max(s, axis=0, keepdims=True) for s in scores])
        return [jnp.exp2(s - top).astype(jnp.bfloat16) for s in scores]

    def summed(weights, values, live):
        total = mix(values, jnp.concatenate(weights, axis=0))
        share = jnp.where(live, 1.0 / total[HEAD : HEAD + 1], 0.0)
        return (total[:HEAD] * share).astype(jnp.bfloat16).T

    copies = []
    ready = weighed(scored(*items[0]))
    ahead = scored(*items[1]) if len(items) > 1 else None
    for n, (r, c, h) in enumerate(items):
        weights, scores = ready, ahead
        if n + 2 < len(items):
            ahead = scored(*items[n + 2])
        if n + 1 < len(items):
            ready = weighed(scores)
        low, high = c * step, (c + 1) * step
        value = all_values[r][:, : prefix_values.shape[1] + high]
        live = low + lax.broadcasted_iota(jnp.int32, (1, step), 1) < len_ref[r]
        result = summed(weights, value, live).astype(jnp.bfloat16)
        hold_ref[r, low:high, h * HEAD : (h + 1) * HEAD] = result
        if h == heads - 1:
            copy = pltpu.make_async_copy(
                hold_ref.at[r, pl.ds(low, step)], out_ref.at[r, pl.ds(low, step)], sems.at[r, c]
            )
            copy.start()
            copies.append(copy)
    for copy in copies:
        copy.wait()


def load_prefix(pieces, pk_ref, pv_ref):
    first = 0
    for p in pieces:
        pk_ref[first : first + p.shape[0], :] = scaled_keys(p[:, :HEAD])
        pv_ref[first : first + p.shape[0], :] = with_ones(p[:, HEAD:])
        first += p.shape[0]


def prefix_kernel(starts_ref, rows_ref, kv_ref, out_ref, pk_ref, pv_ref):
    load_prefix([kv_ref], pk_ref, pv_ref)
    prefix_part(starts_ref, rows_ref, pk_ref, pv_ref, out_ref)


def prefix_call(starts, rows, kv):
    return pl.pallas_call(
        prefix_kernel,
        out_shape=jax.ShapeDtypeStruct((rows.shape[0], rows.shape[1] - 2 * HEAD), jnp.bfloat16),
        in_specs=[SCALARS, WHOLE, WHOLE],
        out_specs=WHOLE,
        scratch_shapes=prefix_scratch(kv.shape[0]),
        compiler_params=pltpu.CompilerParams(vmem_limit_bytes=VMEM_LIMIT),
        cost_estimate=pl.CostEstimate(flops=10**9, bytes_accessed=10**6, transcendentals=0),
        name="prefix_attention",
    )(starts, rows, kv)


def response_kernel(len_ref, order_ref, sent_ref, prefix_ref, *refs):
    blocks = refs[:-7]
    out_ref, arrived_ref, pk_ref, pv_ref, hold_ref, sems, own_sem = refs[-7:]
    responses, slot, span = hold_ref.shape
    index = lax.axis_index("prompt")
    rows_peer = sent_ref.shape[1]
    first = pl.multiple_of(index * rows_peer, rows_peer)
    own = pltpu.make_async_copy(
        sent_ref.at[index], arrived_ref.at[pl.ds(first, rows_peer)], own_sem
    )
    own.start()
    load_prefix([prefix_ref], pk_ref, pv_ref)
    for k, b in enumerate(blocks, 1):
        first = pl.multiple_of((index ^ k) * rows_peer, rows_peer)
        arrived_ref[pl.ds(first, rows_peer), :] = b[...]
    own.wait()
    placed = [place(order_ref, arrived_ref[...], r, slot) for r in range(responses)]
    response_part(
        len_ref,
        [p[:, :span] for p in placed],
        [scaled_keys(p[:, span : span + HEAD]) for p in placed],
        [p[:, span + HEAD :] for p in placed],
        pk_ref,
        pv_ref,
        hold_ref,
        out_ref,
        sems,
    )


WHOLE = pl.BlockSpec(memory_space=pltpu.VMEM)
SCALARS = pl.BlockSpec(memory_space=pltpu.SMEM)
ANYWHERE = pl.BlockSpec(memory_space=pl.ANY)
IN_HBM = pl.BlockSpec(memory_space=pltpu.HBM)


def prefix_scratch(count):
    return [pltpu.VMEM((count, 2 * HEAD), jnp.bfloat16)] * 2


def response_call(lengths, order, sent, prefix_kv, blocks):
    responses = lengths.shape[0]
    slot = order.shape[0] // responses
    feat = sent.shape[2]
    span = feat - 2 * HEAD
    return pl.pallas_call(
        response_kernel,
        out_shape=jax.ShapeDtypeStruct((responses, slot, span), jnp.bfloat16),
        in_specs=[SCALARS, WHOLE, IN_HBM, WHOLE] + [WHOLE] * len(blocks),
        out_specs=ANYWHERE,
        scratch_shapes=[pltpu.VMEM((responses * slot, feat), jnp.bfloat16)]
        + prefix_scratch(prefix_kv.shape[0])
        + [
            pltpu.VMEM((responses, slot, span), jnp.bfloat16),
            pltpu.SemaphoreType.DMA((responses, slot // math.gcd(slot, 256))),
            pltpu.SemaphoreType.DMA,
        ],
        compiler_params=pltpu.CompilerParams(vmem_limit_bytes=VMEM_LIMIT),
        cost_estimate=pl.CostEstimate(flops=5 * 10**9, bytes_accessed=4 * 10**6, transcendentals=0),
        name="response_attention",
    )(lengths, order, sent, prefix_kv, *blocks)


def body(prefix_qkv, rollout, arrival_order, resp_len):
    peers = lax.axis_size("prompt")
    ctx_count = lax.axis_size("ctx")
    ctx_index = lax.axis_index("ctx")
    prefix_rows = prefix_qkv[0]
    prefix_len, feat = prefix_rows.shape
    sent = rollout[0, 0]
    assert peers & (peers - 1) == 0

    def after(value, *done):
        return lax.optimization_barrier((value, *done))[0]

    chips = range(1, peers // 2)
    near = [2 * m for m in chips if m.bit_count() == 1]
    far = [2 * m for m in chips if m.bit_count() > 1]
    pairs = [("pair", k) for k in far]
    evens = [("one", k) for k in near]
    odds = [("one", k + 1) for k in near]
    turns = sorted(range(1, ctx_count), key=lambda t: -min(t, ctx_count - t))
    shifts = [("ctx", t) for t in turns]
    plan = pairs[:1] + evens[:2] + shifts[:2] + shifts[2:] + odds + evens[2:] + pairs[1:]
    plan += [("one", 1)] if peers > 1 else []
    freed = plan[3:5] + plan[:1] * 2 + plan[1:3] + plan[5:]

    def pick(index, step):
        kind, k = step
        if kind == "pair":
            return lax.dynamic_slice_in_dim(sent, (index ^ k) & -2, 2, 0)
        return lax.dynamic_index_in_dim(sent, index ^ k, 0, keepdims=False)

    own_index = lax.axis_index("prompt")
    core = own_index & 1
    swaps = [step for step in plan if step[0] != "ctx"]
    lead = pick(own_index, swaps[0])
    index, rows, lead = lax.optimization_barrier((own_index, prefix_rows, lead))
    picked = {step: pick(index, step) for step in swaps[1:]}
    picked[swaps[0]] = lead
    prefix_kv = rows[:, feat - 2 * HEAD :]

    got, blocks = {}, {}
    for n, step in enumerate(plan):
        kind, by = step
        if kind == "ctx":
            value, route = prefix_kv, [(j, (j + by) % ctx_count) for j in range(ctx_count)]
        else:
            value, route = picked[step], [(j, j ^ by) for j in range(peers)]
        if n >= 5:
            value = after(value, got[freed[n - 5]])
        got[step] = lax.ppermute(value, "ctx" if kind == "ctx" else "prompt", route)
        if kind == "one":
            blocks[by] = got[step]
    for _, k in pairs:
        came = got["pair", k]
        blocks[k] = lax.dynamic_index_in_dim(came, core, 0, keepdims=False)
        other = lax.dynamic_index_in_dim(came, 1 - core, 0, keepdims=False)
        blocks[k + 1] = lax.ppermute(other, "prompt", [(j, j ^ 1) for j in range(peers)])
    blocks = [blocks[k] for k in range(1, peers)]
    prefix_kv = jnp.concatenate([prefix_kv] + [got["ctx", t] for t in range(1, ctx_count)], axis=0)

    order = arrival_order[0, 0].reshape(-1, 1)
    starts = (ctx_index - jnp.arange(ctx_count, dtype=jnp.int32)) % ctx_count * prefix_len
    prefix_out = prefix_call(starts, prefix_rows, prefix_kv)
    resp_out = response_call(
        resp_len[0], order, sent, prefix_kv, blocks
    )
    return (prefix_out[None], resp_out[None])


def solution(mesh):
    placed = (
        P("prompt", "ctx", None),
        P("prompt", "ctx", None, None, None),
        P("prompt", "ctx", None),
        P("prompt", "ctx"),
    )
    return jax.shard_map(
        body,
        mesh=mesh,
        in_specs=placed,
        out_specs=(P("prompt", "ctx", None), P("prompt", "ctx", None, None)),
        check_vma=False,
    )
```
